1024 devices in a mesh: node: 32 (over y_lo, z, core), local: 32 (over y_hi, x).
Axes of the slice: x: 8, y: 8 (y_hi: 4, y_lo: 2; y = y_hi * 2 + y_lo), z: 8, core: 2. Of those that a mesh axis runs over, the one named last changes fastest.
Arguments:
- tokens: bfloat16 [131072, 12288], P(('node', 'local')), may hold values from -6 to 6
- weight_q: bfloat16 [64, 12288], P('local'), may hold values from -127 to 127
- weight_scale: bfloat16 [64, 48], P('local'), may hold values from 6.2942505e-05 to 0.00025177002
- cotangent: bfloat16 [131072, 64], P(('node', 'local')), may hold values from -6 to 6
Outputs:
- activation: bfloat16 [131072, 64], P(('node', 'local'))
- gradient: float32 [3072, 256], P(('node', 'local'))
The draws below stay inside these ranges and needn't reach their ends.
All inputs are finite; a program needn't handle non-finite values. Where the reference program divides by a largest or mean magnitude, that divisor is 1e-20 or more.
Results may differ from the reference program's by a relative error of at most 0.015.
Values may be sent and summed in bfloat16 or wider, within the bound.
No kernel may reach another device: no remote copies, remote signals or barrier semaphores. Data moves between devices by JAX's collectives and lax.ppermute only.
A program may use at most 32 MiB of HBM per device.

```python
import math
import jax
import jax.numpy as jnp
from jax import lax

D = 12288
HB = 64
BLOCK = 256
TOK_DEV = 128
TOKENS = 131072
NBLK = 3072
N_NODE = 32
N_LOCAL = 32


def draw_weight_q(key, part):
    key = jax.random.fold_in(key, 11)
    levels = jax.random.randint(key, (HB, D), -127, 128)
    return levels.astype(jnp.float32).astype(jnp.bfloat16)


def draw_tokens(key, part):
    key = jax.random.fold_in(key, 23)
    column_key, value_key = jax.random.split(key, 2)
    column_scale = jnp.exp(jax.random.uniform(column_key, (D,), jnp.float32, math.log(0.3), math.log(3.0)))
    entries = jax.random.truncated_normal(value_key, -2.0, 2.0, (TOKENS, D), jnp.float32)
    return (entries * column_scale[None, :]).astype(jnp.bfloat16)


def steps_of(own_key, dims, pieces, least, top_value):
    gain, own = 1.0, jax.random.fold_in(own_key, 6)
    for axis_at, blocks in pieces:
        draws = jnp.exp(jax.random.uniform(jax.random.fold_in(own, axis_at), (blocks,), jnp.float32, least / len(pieces), top_value / len(pieces)))
        gain = gain * jnp.repeat(draws, dims[axis_at] // blocks).reshape([-1 if axis == axis_at else 1 for axis in range(len(dims))])
    return gain


def noise(key, extent, spread, reach, shards=(), held_as=jnp.bfloat16):
    gain = steps_of(key, extent, shards, -0.22, 0.18) if shards else 1.0
    values = jax.random.normal(key, extent, jnp.float32) * spread * gain
    return jnp.minimum(jnp.maximum(values, -reach), reach).astype(held_as)


def setup_inputs(seed: int = 0) -> dict:
    streams_of = jax.random.split(jax.random.key(seed), 5)
    tokens = draw_tokens(jax.random.fold_in(streams_of[4], 71), 0)
    weight_q = draw_weight_q(jax.random.fold_in(streams_of[4], 71), 0)
    weight_scale = jnp.clip(jnp.exp(math.log(0.00025177002) - 1.3862944 * jax.random.uniform(streams_of[2], (HB, D // BLOCK), jnp.float32) ** steps_of(streams_of[2], (HB, D // BLOCK), ((0, 32),), -0.2, 0.2)), 6.29425048828125e-05, 0.00025177002).astype(jnp.bfloat16)
    cotangent = noise(streams_of[3], (TOKENS, HB), 1.0, 6.0, ((0, 1024),))
    return {"tokens": tokens, "weight_q": weight_q, "weight_scale": weight_scale, "cotangent": cotangent}


EPSILON = 1e-6
CLIP_LEVEL = 3.0
TANH_SCALE = 0.7978845608028654
CUBIC_TERM = 0.044715


def gelu_value(before):
    inner = TANH_SCALE * (before + CUBIC_TERM * before * before * before)
    return 0.5 * before * (1.0 + jnp.tanh(inner))


def gelu_slope(before):
    tanh_inner = jnp.tanh(TANH_SCALE * (before + CUBIC_TERM * before * before * before))
    return 0.5 * (1.0 + tanh_inner) + 0.5 * before * (1.0 - tanh_inner * tanh_inner) * TANH_SCALE * (1.0 + 3.0 * CUBIC_TERM * before * before)


def quantize(blocks):
    scales = (jnp.mean(jnp.abs(blocks), axis=-1) + EPSILON).astype(jnp.bfloat16)
    ratios = blocks / scales.astype(jnp.float32)[..., None]
    quants = jnp.clip(ratios, -CLIP_LEVEL, CLIP_LEVEL).astype(jnp.bfloat16)
    return quants, scales


def dequantize(quants, scales):
    return quants.astype(jnp.float32) * scales.astype(jnp.float32)[..., None]


def reference(tokens, weight_q, weight_scale, cotangent):
    weight = (weight_q.astype(jnp.float32) * jnp.repeat(weight_scale.astype(jnp.float32), BLOCK, axis=1)).astype(jnp.bfloat16)
    before = jnp.dot(tokens, weight.T, preferred_element_type=jnp.float32)
    activation = gelu_value(before).astype(jnp.bfloat16)
    slope_term = (cotangent.astype(jnp.float32) * gelu_slope(before)).astype(jnp.bfloat16)
    token_groups = tokens.reshape(N_NODE, N_LOCAL, TOK_DEV, D)
    slope_groups = slope_term.reshape(N_NODE, N_LOCAL, TOK_DEV, HB)

    def member(member_tokens, member_slopes):
        partial_value = lax.dot_general(member_slopes, member_tokens, (((0,), (0,)), ((), ())), preferred_element_type=jnp.float32)
        quants, scales = quantize(partial_value.reshape(NBLK, BLOCK))
        return dequantize(quants, scales)

    def group_step(summed, inputs):
        group_tokens, group_slopes = inputs
        group = jnp.sum(jax.vmap(member)(group_tokens, group_slopes), axis=0)
        quants, scales = quantize(group)
        return summed + dequantize(quants, scales), None

    gradient, unused = lax.scan(group_step, jnp.zeros((NBLK, BLOCK), jnp.float32), (token_groups, slope_groups))
    return activation, gradient
```

```python
import jax
import jax.numpy as jnp
from jax import lax
from jax.experimental import pallas as pl
from jax.experimental.pallas import tpu as pltpu
from jax.sharding import PartitionSpec as P

BLOCK = 256
EPSILON = 1e-06
CLIP_LEVEL = 3.0
TANH_SCALE = 0.7978845608028654
CUBIC_TERM = 0.044715
SUB = 16
VMEM_LIMIT = 48 * 1024 * 1024


def clip_blocks(values):
    parts = []
    for k in range(values.shape[1] // BLOCK):
        block = values[:, k * BLOCK : (k + 1) * BLOCK]
        mean = jnp.sum(jnp.abs(block), axis=1, keepdims=True) * (1.0 / BLOCK)
        scale = (mean + EPSILON).astype(jnp.bfloat16).astype(jnp.float32)
        bound = CLIP_LEVEL * scale
        parts.append(jnp.minimum(jnp.maximum(block, -bound), bound))
    return jnp.concatenate(parts, axis=1)


def gradient_kernel(half_ref, tokens_ref, own_ref, other_ref, cot_ref, act_ref, out_ref):
    width = own_ref.shape[2]
    rows = own_ref.shape[0] * SUB
    cols = SUB // 2
    batch = tokens_ref.shape[0]
    which = lax.broadcasted_iota(jnp.int32, (rows, 1), 0) % cols
    total = jnp.zeros((rows, batch), jnp.float32)
    for part, ref in enumerate((own_ref, other_ref)):
        start = (half_ref[0] if part == 0 else 1 - half_ref[0]) * (cols * width)
        weight = ref[...].reshape(rows, width)
        for c in range(cols):
            columns = pl.ds(pl.multiple_of(start + c * width, 128), width)
            product = lax.dot_general(
                weight, tokens_ref[:, columns], (((1,), (1,)), ((), ())), preferred_element_type=jnp.float32
            )
            total = total + jnp.where(which == c, product, 0.0)
    before = jnp.sum(total.reshape(rows // cols, cols, batch), axis=1)

    tanh_inner = jnp.tanh(TANH_SCALE * (before + CUBIC_TERM * before * before * before))
    act = 0.5 * before * (1.0 + tanh_inner)
    act_ref[...] = act.T.astype(jnp.bfloat16)
    slope = 0.5 * (1.0 + tanh_inner) + 0.5 * before * (1.0 - tanh_inner * tanh_inner) * TANH_SCALE * (
        1.0 + 3.0 * CUBIC_TERM * before * before
    )
    slope = (cot_ref[...].astype(jnp.float32).T * slope).astype(jnp.bfloat16)
    hidden = slope.shape[0]
    to = lax.broadcasted_iota(jnp.int32, (hidden, hidden), 0)
    source = lax.broadcasted_iota(jnp.int32, (hidden, hidden), 1)
    pick = source == (to % (hidden // 2)) * 2 + to // (hidden // 2)
    slope = jnp.dot(
        jnp.where(pick, 1.0, 0.0).astype(jnp.bfloat16), slope, preferred_element_type=jnp.float32
    ).astype(jnp.bfloat16)

    slots, nodes, piece = out_ref.shape
    for i in range(slots // 2):
        partial = jnp.dot(slope, tokens_ref[:, i * piece : (i + 1) * piece], preferred_element_type=jnp.float32)
        value = clip_blocks(partial).astype(jnp.bfloat16)
        out_ref[i] = value[:nodes]
        out_ref[slots // 2 + i] = value[nodes:]


def group_kernel(parts_ref, out_ref):
    total = parts_ref[0].astype(jnp.float32)
    for i in range(1, parts_ref.shape[0]):
        total = total + parts_ref[i].astype(jnp.float32)
    out_ref[...] = clip_blocks(total).astype(jnp.bfloat16)


def per_device(tokens, weight_q, weight_scale, cotangent):
    node_count = lax.axis_size("node")
    local_count = lax.axis_size("local")
    batch, depth = tokens.shape
    own_rows = weight_q.shape[0]
    hidden = cotangent.shape[1]
    half = lax.axis_index("node") % 2
    piece = hidden * depth // (node_count * local_count)

    weight = (
        weight_q.astype(jnp.float32) * jnp.repeat(weight_scale.astype(jnp.float32), BLOCK, axis=1)
    ).astype(jnp.bfloat16)
    mine = lax.dynamic_slice_in_dim(weight, half * (depth // 2), depth // 2, axis=1)
    mine = mine.reshape(SUB, own_rows * depth // 2 // SUB)
    copies = jnp.broadcast_to(mine[None], (local_count,) + mine.shape)
    own = lax.all_to_all(copies, "local", split_axis=0, concat_axis=0, tiled=True)
    other = lax.ppermute(own, "node", [(n, n ^ 1) for n in range(node_count)])

    vmem = pl.BlockSpec(memory_space=pltpu.VMEM)
    activation, sent = pl.pallas_call(
        gradient_kernel,
        out_shape=(
            jax.ShapeDtypeStruct((batch, hidden), jnp.bfloat16),
            jax.ShapeDtypeStruct((local_count, node_count, piece), jnp.bfloat16),
        ),
        in_specs=[pl.BlockSpec(memory_space=pltpu.SMEM)] + [vmem] * 4,
        out_specs=(vmem, vmem),
        compiler_params=pltpu.CompilerParams(vmem_limit_bytes=VMEM_LIMIT),
    )(half.astype(jnp.int32).reshape(1), tokens, own, other, cotangent)

    got = lax.all_to_all(sent, "local", split_axis=0, concat_axis=0, tiled=True)
    group = pl.pallas_call(
        group_kernel,
        out_shape=jax.ShapeDtypeStruct((node_count, piece), jnp.bfloat16),
        in_specs=[vmem],
        out_specs=vmem,
        compiler_params=pltpu.CompilerParams(vmem_limit_bytes=VMEM_LIMIT),
    )(got)
    group = group.reshape(node_count, piece // BLOCK, BLOCK)
    got = lax.all_to_all(group, "node", split_axis=0, concat_axis=0, tiled=True)
    gradient = jnp.sum(got.astype(jnp.float32), axis=0)
    return (activation, gradient)


def solution(mesh):
    return jax.shard_map(
        per_device,
        mesh=mesh,
        in_specs=(
            P(("node", "local"), None),
            P("local", None),
            P("local", None),
            P(("node", "local"), None),
        ),
        out_specs=(P(("node", "local"), None), P(("node", "local"), None)),
        check_vma=False,
    )
```

```python
import functools

import jax
import jax.numpy as jnp
from jax import lax
from jax.experimental import pallas as pl
from jax.experimental.pallas import tpu as pltpu
from jax.sharding import Mesh, PartitionSpec as P

BLOCK = 256
EPSILON = 1e-06
CLIP_LEVEL = 3.0
TANH_SCALE = 0.7978845608028654
CUBIC_TERM = 0.044715
ROWS = 16
RING_Y, RING_X = 4, 8
PARAMS = pltpu.CompilerParams(vmem_limit_bytes=24 * 1024 * 1024)
VMEM = pl.BlockSpec(memory_space=pltpu.VMEM)
SMEM = pl.BlockSpec(memory_space=pltpu.SMEM)


def shape(dims, dtype=jnp.bfloat16):
    return jax.ShapeDtypeStruct(dims, dtype)


def clip_block(block):
    mean = jnp.sum(jnp.abs(block), axis=1, keepdims=True) * (1.0 / BLOCK)
    scale = (mean + EPSILON).astype(jnp.bfloat16).astype(jnp.float32)
    bound = CLIP_LEVEL * scale
    return jnp.minimum(jnp.maximum(block, -bound), bound).astype(jnp.bfloat16)


def clip_blocks(values):
    return jnp.concatenate(
        [clip_block(values[:, k : k + BLOCK]) for k in range(0, values.shape[1], BLOCK)], axis=1
    )


def weight_kernel(half_ref, quant_ref, scale_ref, out_ref):
    own_rows, depth = quant_ref.shape
    width = out_ref.shape[2]
    pieces = depth // 2 // width
    first = half_ref[0] == 0
    scales = scale_ref[...].astype(jnp.float32)
    rows = []
    for r in range(own_rows):
        for c in range(pieces):
            halves = []
            for start in (c * width, depth // 2 + c * width):
                quant = quant_ref[r : r + 1, start : start + width].astype(jnp.float32)
                spread = [
                    jnp.broadcast_to(scales[r : r + 1, k : k + 1], (1, BLOCK))
                    for k in range(start // BLOCK, (start + width) // BLOCK)
                ]
                halves.append(quant * jnp.concatenate(spread, axis=1))
            rows.append(jnp.where(first, halves[0], halves[1]))
    weight = jnp.concatenate(rows, axis=0).astype(jnp.bfloat16)
    for slot in range(out_ref.shape[0]):
        out_ref[slot] = weight


def before_half(half, tokens_ref, rows_ref):
    batch = tokens_ref.shape[0]
    count, width = rows_ref.shape[0] * ROWS, rows_ref.shape[2]
    pieces = ROWS // 2
    weight = rows_ref[...].reshape(count, width)
    which = lax.broadcasted_iota(jnp.int32, (count, 1), 0) % pieces
    total = jnp.zeros((count, batch), jnp.float32)
    for c in range(0, pieces, 2):
        pair = [
            tokens_ref[:, pl.ds(pl.multiple_of((half * pieces + c + k) * width, 128), width)] for k in range(2)
        ]
        product = lax.dot_general(
            weight, jnp.concatenate(pair, axis=0), (((1,), (1,)), ((), ())), preferred_element_type=jnp.float32
        )
        total = total + jnp.where(which == c, product[:, :batch], 0.0)
        total = total + jnp.where(which == c + 1, product[:, batch:], 0.0)
    return jnp.sum(total.reshape(count // pieces, pieces, batch), axis=1)


def own_kernel(half_ref, tokens_ref, rows_ref, out_ref):
    out_ref[...] = before_half(half_ref[0], tokens_ref, rows_ref)


def first_kernel(half_ref, tokens_ref, rows_ref, own_ref, cot_ref, act_ref, sent_ref):
    before = own_ref[...] + before_half(1 - half_ref[0], tokens_ref, rows_ref)
    tanh_inner = jnp.tanh(TANH_SCALE * (before + CUBIC_TERM * before * before * before))
    act_ref[...] = (0.5 * before * (1.0 + tanh_inner)).astype(jnp.bfloat16)
    slope = 0.5 * (1.0 + tanh_inner) + 0.5 * before * (1.0 - tanh_inner * tanh_inner) * TANH_SCALE * (
        1.0 + 3.0 * CUBIC_TERM * before * before
    )
    slope = (cot_ref[...].astype(jnp.float32) * slope).astype(jnp.bfloat16)
    hidden = slope.shape[0]
    to = lax.broadcasted_iota(jnp.int32, (hidden, hidden), 0)
    source = lax.broadcasted_iota(jnp.int32, (hidden, hidden), 1)
    pick = source == to % (hidden // 2) * 2 + to // (hidden // 2)
    slope = jnp.dot(
        jnp.where(pick, 1.0, 0.0).astype(jnp.bfloat16), slope, preferred_element_type=jnp.float32
    ).astype(jnp.bfloat16)
    nodes = slope.shape[0] // 2
    per_row = RING_Y * RING_X // 2
    piece = tokens_ref.shape[1] // per_row
    for i in range(per_row):
        partial = jnp.dot(slope, tokens_ref[:, i * piece : (i + 1) * piece], preferred_element_type=jnp.float32)
        value = clip_blocks(partial)
        for row_parity in range(2):
            owner = row_parity * per_row + i
            sent_ref[owner] = value[row_parity * nodes : (row_parity + 1) * nodes]


def group_kernel(got_ref, out_ref):
    total = got_ref[0].astype(jnp.float32)
    for i in range(1, got_ref.shape[0]):
        total = total + got_ref[i].astype(jnp.float32)
    for k in range(out_ref.shape[1]):
        out_ref[:, k, :] = clip_block(total[:, k * BLOCK : (k + 1) * BLOCK])


def per_device(tokens, weight_q, weight_scale, cotangent):
    node_count = lax.axis_size("node")
    local_count = RING_Y * RING_X
    batch, depth = tokens.shape
    own_rows = weight_q.shape[0]
    hidden = cotangent.shape[1]
    piece = hidden * depth // (node_count * local_count)
    side = node_count // 2
    half = (lax.axis_index("node") % 2).astype(jnp.int32).reshape(1)
    parity = lax.axis_index("parity").astype(jnp.int32).reshape(1)
    call = functools.partial(pl.pallas_call, compiler_params=PARAMS)

    share = shape((local_count, ROWS, own_rows * depth // 2 // ROWS))
    copies = call(weight_kernel, out_shape=share, in_specs=[SMEM, VMEM, VMEM], out_specs=VMEM)(
        half, weight_q, weight_scale
    )
    own = lax.all_to_all(copies, ("y", "pair", "parity"), split_axis=0, concat_axis=0, tiled=True)
    other = lax.ppermute(own, "node", [(n, n ^ 1) for n in range(node_count)])
    before = call(
        own_kernel, out_shape=shape((hidden, batch), jnp.float32), in_specs=[SMEM, VMEM, VMEM], out_specs=VMEM
    )(half, tokens, own)
    activation, sent = call(
        first_kernel,
        out_shape=(shape((hidden, batch)), shape((local_count, node_count, piece))),
        in_specs=[SMEM] + [VMEM] * 4,
        out_specs=(VMEM,) * 2,
    )(half, tokens, other, before, cotangent.T)
    got = lax.all_to_all(sent, ("y", "pair", "parity"), split_axis=0, concat_axis=0, tiled=True)
    group = call(
        group_kernel, out_shape=shape((node_count, piece // BLOCK, BLOCK)), in_specs=[VMEM], out_specs=VMEM
    )(got)
    got = lax.all_to_all(group, "node", split_axis=0, concat_axis=0, tiled=True)
    gradient = jnp.sum(got.astype(jnp.float32), axis=0)
    return (activation.T, gradient)


def solution(mesh):
    axes = ("node", "y", "pair", "parity")
    fine = Mesh(mesh.devices.reshape(mesh.devices.shape[0], RING_Y, RING_X // 2, 2), axes)
    everywhere, group = P(axes, None), P(axes[1:], None)
    return jax.shard_map(
        per_device,
        mesh=fine,
        in_specs=(everywhere, group, group, everywhere),
        out_specs=(everywhere, everywhere),
        check_vma=False,
    )
```

```python
import functools

import jax
import jax.numpy as jnp
from jax import lax
from jax.experimental import pallas as pl
from jax.experimental.pallas import tpu as pltpu
from jax.sharding import Mesh, PartitionSpec as P

BLOCK = 256
EPSILON = 1e-06
CLIP_LEVEL = 3.0
TANH_SCALE = 0.7978845608028654
CUBIC_TERM = 0.044715
ROWS = 16
RING_Y, RING_X = 4, 8
PARAMS = pltpu.CompilerParams(vmem_limit_bytes=24 * 1024 * 1024)
VMEM = pl.BlockSpec(memory_space=pltpu.VMEM)
SMEM = pl.BlockSpec(memory_space=pltpu.SMEM)


def shape(dims, dtype=jnp.bfloat16):
    return jax.ShapeDtypeStruct(dims, dtype)


def clip_block(block):
    mean = jnp.sum(jnp.abs(block), axis=1, keepdims=True) * (1.0 / BLOCK)
    scale = (mean + EPSILON).astype(jnp.bfloat16).astype(jnp.float32)
    bound = CLIP_LEVEL * scale
    return jnp.minimum(jnp.maximum(block, -bound), bound).astype(jnp.bfloat16)


def clip_blocks(values):
    return jnp.concatenate(
        [clip_block(values[:, k : k + BLOCK]) for k in range(0, values.shape[1], BLOCK)], axis=1
    )


def weight_kernel(half_ref, quant_ref, scale_ref, out_ref):
    own_rows, depth = quant_ref.shape
    width = out_ref.shape[2]
    pieces = depth // 2 // width
    first = half_ref[0] == 0
    scales = scale_ref[...].astype(jnp.float32)
    rows = []
    for r in range(own_rows):
        for c in range(pieces):
            halves = []
            for start in (c * width, depth // 2 + c * width):
                quant = quant_ref[r : r + 1, start : start + width].astype(jnp.float32)
                spread = [
                    jnp.broadcast_to(scales[r : r + 1, k : k + 1], (1, BLOCK))
                    for k in range(start // BLOCK, (start + width) // BLOCK)
                ]
                halves.append(quant * jnp.concatenate(spread, axis=1))
            rows.append(jnp.where(first, halves[0], halves[1]))
    weight = jnp.concatenate(rows, axis=0).astype(jnp.bfloat16)
    for slot in range(out_ref.shape[0]):
        out_ref[slot] = weight


def before_half(half, tokens_ref, rows_ref):
    batch = tokens_ref.shape[0]
    count, width = rows_ref.shape[0] * ROWS, rows_ref.shape[2]
    pieces = ROWS // 2
    weight = rows_ref[...].reshape(count, width)
    which = lax.broadcasted_iota(jnp.int32, (count, 1), 0) % pieces
    total = jnp.zeros((count, batch), jnp.float32)
    for c in range(0, pieces, 2):
        pair = [
            tokens_ref[:, pl.ds(pl.multiple_of((half * pieces + c + k) * width, 128), width)] for k in range(2)
        ]
        product = lax.dot_general(
            weight, jnp.concatenate(pair, axis=0), (((1,), (1,)), ((), ())), preferred_element_type=jnp.float32
        )
        total = total + jnp.where(which == c, product[:, :batch], 0.0)
        total = total + jnp.where(which == c + 1, product[:, batch:], 0.0)
    return jnp.sum(total.reshape(count // pieces, pieces, batch), axis=1)


def own_kernel(half_ref, tokens_ref, rows_ref, out_ref):
    out_ref[...] = before_half(half_ref[0], tokens_ref, rows_ref)


def first_kernel(half_ref, parity_ref, tokens_ref, rows_ref, own_ref, cot_ref, act_ref, sent_ref):
    before = own_ref[...] + before_half(1 - half_ref[0], tokens_ref, rows_ref)
    tanh_inner = jnp.tanh(TANH_SCALE * (before + CUBIC_TERM * before * before * before))
    act_ref[...] = (0.5 * before * (1.0 + tanh_inner)).astype(jnp.bfloat16)
    slope = 0.5 * (1.0 + tanh_inner) + 0.5 * before * (1.0 - tanh_inner * tanh_inner) * TANH_SCALE * (
        1.0 + 3.0 * CUBIC_TERM * before * before
    )
    slope = (cot_ref[...].astype(jnp.float32) * slope).astype(jnp.bfloat16)
    hidden = slope.shape[0]
    to = lax.broadcasted_iota(jnp.int32, (hidden, hidden), 0)
    source = lax.broadcasted_iota(jnp.int32, (hidden, hidden), 1)
    pick = source == to % (hidden // 2) * 2 + to // (hidden // 2)
    slope = jnp.dot(
        jnp.where(pick, 1.0, 0.0).astype(jnp.bfloat16), slope, preferred_element_type=jnp.float32
    ).astype(jnp.bfloat16)
    slots, nodes, piece = sent_ref.shape[1:]
    for i in range(slots):
        partial = jnp.dot(slope, tokens_ref[:, i * piece : (i + 1) * piece], preferred_element_type=jnp.float32)
        value = clip_blocks(partial)
        for row_parity in range(2):
            owner = row_parity * slots + i
            sent_ref[(owner + parity_ref[0]) % 2, owner // 2] = value[row_parity * nodes : (row_parity + 1) * nodes]


def pair_kernel(kept_ref, got_ref, out_ref):
    for slot in range(out_ref.shape[0]):
        total = kept_ref[0, slot].astype(jnp.float32) + got_ref[slot].astype(jnp.float32)
        out_ref[slot] = total.astype(jnp.bfloat16)


def group_kernel(got_ref, out_ref):
    total = got_ref[0].astype(jnp.float32)
    for i in range(1, got_ref.shape[0]):
        total = total + got_ref[i].astype(jnp.float32)
    for k in range(out_ref.shape[1]):
        out_ref[:, k, :] = clip_block(total[:, k * BLOCK : (k + 1) * BLOCK])


def per_device(tokens, weight_q, weight_scale, cotangent):
    node_count = lax.axis_size("node")
    local_count = RING_Y * RING_X
    batch, depth = tokens.shape
    own_rows = weight_q.shape[0]
    hidden = cotangent.shape[1]
    piece = hidden * depth // (node_count * local_count)
    half = (lax.axis_index("node") % 2).astype(jnp.int32).reshape(1)
    parity = lax.axis_index("parity").astype(jnp.int32).reshape(1)
    call = functools.partial(pl.pallas_call, compiler_params=PARAMS)

    share = shape((local_count, ROWS, own_rows * depth // 2 // ROWS))
    copies = call(weight_kernel, out_shape=share, in_specs=[SMEM, VMEM, VMEM], out_specs=VMEM)(
        half, weight_q, weight_scale
    )
    own = lax.all_to_all(copies, ("y", "pair", "parity"), split_axis=0, concat_axis=0, tiled=True)
    other = lax.ppermute(own, "node", [(n, n ^ 1) for n in range(node_count)])
    before = call(
        own_kernel, out_shape=shape((hidden, batch), jnp.float32), in_specs=[SMEM, VMEM, VMEM], out_specs=VMEM
    )(half, tokens, own)
    activation, parts = call(
        first_kernel,
        out_shape=(shape((hidden, batch)), shape((2, local_count // 2, node_count, piece))),
        in_specs=[SMEM] * 2 + [VMEM] * 4,
        out_specs=(VMEM,) * 2,
    )(half, parity, tokens, other, before, cotangent.T)
    partners = [
        (n * RING_X + x, n * RING_X + (x + (1 if (x + n) % 2 == 0 else -1)) % RING_X)
        for n in range(node_count)
        for x in range(RING_X)
    ]
    paired = lax.ppermute(parts[1], ("node", "pair", "parity"), partners)
    sent = call(
        pair_kernel, out_shape=shape((local_count // 2, node_count, piece)), in_specs=[VMEM] * 2, out_specs=VMEM
    )(parts, paired)
    got = lax.all_to_all(sent, ("y", "pair"), split_axis=0, concat_axis=0, tiled=True)
    group = call(
        group_kernel, out_shape=shape((node_count, piece // BLOCK, BLOCK)), in_specs=[VMEM], out_specs=VMEM
    )(got)
    got = lax.all_to_all(group, "node", split_axis=0, concat_axis=0, tiled=True)
    gradient = jnp.sum(got.astype(jnp.float32), axis=0)
    return (activation.T, gradient)


def solution(mesh):
    axes = ("node", "y", "pair", "parity")
    fine = Mesh(mesh.devices.reshape(mesh.devices.shape[0], RING_Y, RING_X // 2, 2), axes)
    everywhere, group = P(axes, None), P(axes[1:], None)
    return jax.shard_map(
        per_device,
        mesh=fine,
        in_specs=(everywhere, group, group, everywhere),
        out_specs=(everywhere, everywhere),
        check_vma=False,
    )
```

```python
import functools

import jax
import jax.numpy as jnp
from jax import lax
from jax.experimental import pallas as pl
from jax.experimental.pallas import tpu as pltpu
from jax.sharding import Mesh, PartitionSpec as P

BLOCK = 256
EPSILON = 1e-06
CLIP_LEVEL = 3.0
TANH_SCALE = 0.7978845608028654
CUBIC_TERM = 0.044715
ROWS = 16
RING_Y, RING_X = 4, 8
PARAMS = pltpu.CompilerParams(vmem_limit_bytes=24 * 1024 * 1024)
VMEM = pl.BlockSpec(memory_space=pltpu.VMEM)
SMEM = pl.BlockSpec(memory_space=pltpu.SMEM)
HBM = pl.BlockSpec(memory_space=pltpu.HBM)


def shape(dims, dtype=jnp.bfloat16):
    return jax.ShapeDtypeStruct(dims, dtype)


def in_hbm(value):
    return pltpu.with_memory_space_constraint(value, pltpu.HBM)


def clip_block(block):
    mean = jnp.sum(jnp.abs(block), axis=1, keepdims=True) * (1.0 / BLOCK)
    scale = (mean + EPSILON).astype(jnp.bfloat16).astype(jnp.float32)
    bound = CLIP_LEVEL * scale
    return jnp.minimum(jnp.maximum(block, -bound), bound).astype(jnp.bfloat16)


def clip_blocks(values):
    return jnp.concatenate(
        [clip_block(values[:, k : k + BLOCK]) for k in range(0, values.shape[1], BLOCK)], axis=1
    )


def weight_kernel(half_ref, quant_hbm, scale_hbm, out_ref, quant_ref, scale_ref, sems):
    fetches = [
        pltpu.make_async_copy(quant_hbm, quant_ref, sems.at[0]),
        pltpu.make_async_copy(scale_hbm, scale_ref, sems.at[1]),
    ]
    for fetch in fetches:
        fetch.start()
    for fetch in fetches:
        fetch.wait()
    own_rows, depth = quant_ref.shape
    width = out_ref.shape[2]
    pieces = depth // 2 // width
    first = half_ref[0] == 0
    scales = scale_ref[...].astype(jnp.float32)
    rows = []
    for r in range(own_rows):
        for c in range(pieces):
            halves = []
            for start in (c * width, depth // 2 + c * width):
                quant = quant_ref[r : r + 1, start : start + width].astype(jnp.float32)
                spread = [
                    jnp.broadcast_to(scales[r : r + 1, k : k + 1], (1, BLOCK))
                    for k in range(start // BLOCK, (start + width) // BLOCK)
                ]
                halves.append(quant * jnp.concatenate(spread, axis=1))
            rows.append(jnp.where(first, halves[0], halves[1]))
    weight = jnp.concatenate(rows, axis=0).astype(jnp.bfloat16)
    for slot in range(out_ref.shape[0]):
        out_ref[slot] = weight


def before_half(half, tokens_ref, rows_ref):
    batch = tokens_ref.shape[0]
    count, width = rows_ref.shape[0] * ROWS, rows_ref.shape[2]
    pieces = ROWS // 2
    weight = rows_ref[...].reshape(count, width)
    which = lax.broadcasted_iota(jnp.int32, (count, 1), 0) % pieces
    total = jnp.zeros((count, batch), jnp.float32)
    for c in range(0, pieces, 2):
        pair = [
            tokens_ref[:, pl.ds(pl.multiple_of((half * pieces + c + k) * width, 128), width)] for k in range(2)
        ]
        product = lax.dot_general(
            weight, jnp.concatenate(pair, axis=0), (((1,), (1,)), ((), ())), preferred_element_type=jnp.float32
        )
        total = total + jnp.where(which == c, product[:, :batch], 0.0)
        total = total + jnp.where(which == c + 1, product[:, batch:], 0.0)
    return jnp.sum(total.reshape(count // pieces, pieces, batch), axis=1)


def own_kernel(half_ref, tokens_ref, rows_ref, out_ref):
    out_ref[...] = before_half(half_ref[0], tokens_ref, rows_ref)


def first_kernel(half_ref, parity_ref, tokens_ref, rows_ref, own_ref, cot_ref, act_ref, slope_ref, sent_ref):
    before = own_ref[...] + before_half(1 - half_ref[0], tokens_ref, rows_ref)
    tanh_inner = jnp.tanh(TANH_SCALE * (before + CUBIC_TERM * before * before * before))
    act_ref[...] = (0.5 * before * (1.0 + tanh_inner)).astype(jnp.bfloat16)
    slope = 0.5 * (1.0 + tanh_inner) + 0.5 * before * (1.0 - tanh_inner * tanh_inner) * TANH_SCALE * (
        1.0 + 3.0 * CUBIC_TERM * before * before
    )
    slope = (cot_ref[...].astype(jnp.float32) * slope).astype(jnp.bfloat16)
    hidden = slope.shape[0]
    to = lax.broadcasted_iota(jnp.int32, (hidden, hidden), 0)
    source = lax.broadcasted_iota(jnp.int32, (hidden, hidden), 1)
    pick = source == to % (hidden // 2) * 2 + to // (hidden // 2)
    slope = jnp.dot(
        jnp.where(pick, 1.0, 0.0).astype(jnp.bfloat16), slope, preferred_element_type=jnp.float32
    ).astype(jnp.bfloat16)
    slope_ref[...] = slope
    partials(slope, tokens_ref, 1 - parity_ref[0], sent_ref)


def second_kernel(parity_ref, tokens_ref, slope_ref, kept_ref):
    partials(slope_ref[...], tokens_ref, parity_ref[0], kept_ref)


def partials(slope, tokens_ref, parity, out_ref):
    slots, nodes, piece = out_ref.shape
    for i in range(slots // 2):
        columns = pl.ds(pl.multiple_of((2 * i + parity) * piece, 128), piece)
        partial = jnp.dot(slope, tokens_ref[:, columns], preferred_element_type=jnp.float32)
        value = clip_blocks(partial)
        out_ref[i] = value[:nodes]
        out_ref[slots // 2 + i] = value[nodes:]


def pair_kernel(kept_ref, got_ref, out_ref):
    for slot in range(out_ref.shape[0]):
        total = kept_ref[slot].astype(jnp.float32) + got_ref[slot].astype(jnp.float32)
        out_ref[slot] = total.astype(jnp.bfloat16)


def group_kernel(got_ref, out_ref):
    total = got_ref[0].astype(jnp.float32)
    for i in range(1, got_ref.shape[0]):
        total = total + got_ref[i].astype(jnp.float32)
    for k in range(out_ref.shape[1]):
        out_ref[:, k, :] = clip_block(total[:, k * BLOCK : (k + 1) * BLOCK])


def per_device(tokens, weight_q, weight_scale, cotangent):
    node_count = lax.axis_size("node")
    local_count = RING_Y * RING_X
    batch, depth = tokens.shape
    own_rows = weight_q.shape[0]
    hidden = cotangent.shape[1]
    piece = hidden * depth // (node_count * local_count)
    half = (lax.axis_index("node") % 2).astype(jnp.int32).reshape(1)
    parity = lax.axis_index("parity").astype(jnp.int32).reshape(1)
    call = functools.partial(pl.pallas_call, compiler_params=PARAMS)

    tokens = pltpu.with_memory_space_constraint(tokens, pltpu.VMEM)
    share = shape((local_count, ROWS, own_rows * depth // 2 // ROWS))
    copies = call(
        weight_kernel,
        out_shape=share,
        in_specs=[SMEM, HBM, HBM],
        out_specs=VMEM,
        scratch_shapes=[
            pltpu.VMEM(weight_q.shape, weight_q.dtype),
            pltpu.VMEM(weight_scale.shape, weight_scale.dtype),
            pltpu.SemaphoreType.DMA((2,)),
        ],
    )(half, in_hbm(weight_q), in_hbm(weight_scale))
    own = lax.all_to_all(copies, ("y", "pair", "parity"), split_axis=0, concat_axis=0, tiled=True)
    other = lax.ppermute(own, "node", [(n, n ^ 1) for n in range(node_count)])
    before = call(
        own_kernel, out_shape=shape((hidden, batch), jnp.float32), in_specs=[SMEM, VMEM, VMEM], out_specs=VMEM
    )(half, tokens, own)
    parts = shape((local_count // 2, node_count, piece))
    activation, slope, sent = call(
        first_kernel,
        out_shape=(shape((hidden, batch)), shape((hidden, batch)), parts),
        in_specs=[SMEM] * 2 + [VMEM] * 4,
        out_specs=(VMEM,) * 3,
    )(half, parity, tokens, other, before, cotangent.T)
    kept = call(second_kernel, out_shape=parts, in_specs=[SMEM, VMEM, VMEM], out_specs=VMEM)(parity, tokens, slope)
    partners = [
        (n * RING_X + x, n * RING_X + (x + (1 if (x + n) % 2 == 0 else -1)) % RING_X)
        for n in range(node_count)
        for x in range(RING_X)
    ]
    paired = lax.ppermute(sent, ("node", "pair", "parity"), partners)
    sent = call(
        pair_kernel, out_shape=parts, in_specs=[VMEM] * 2, out_specs=VMEM
    )(kept, paired)
    got = lax.all_to_all(sent, ("y", "pair"), split_axis=0, concat_axis=0, tiled=True)
    group = call(
        group_kernel, out_shape=shape((node_count, piece // BLOCK, BLOCK)), in_specs=[VMEM], out_specs=VMEM
    )(got)
    got = lax.all_to_all(group, "node", split_axis=0, concat_axis=0, tiled=True)
    gradient = jnp.sum(got.astype(jnp.float32), axis=0)
    return (activation.T, gradient)


def solution(mesh):
    axes = ("node", "y", "pair", "parity")
    fine = Mesh(mesh.devices.reshape(mesh.devices.shape[0], RING_Y, RING_X // 2, 2), axes)
    everywhere, group = P(axes, None), P(axes[1:], None)
    return jax.shard_map(
        per_device,
        mesh=fine,
        in_specs=(everywhere, group, group, everywhere),
        out_specs=(everywhere, everywhere),
        check_vma=False,
    )
```

```python
import functools

import jax
import jax.numpy as jnp
from jax import lax
from jax.experimental import pallas as pl
from jax.experimental.pallas import tpu as pltpu
from jax.sharding import Mesh, PartitionSpec as P

BLOCK = 256
EPSILON = 1e-06
CLIP_LEVEL = 3.0
TANH_SCALE = 0.7978845608028654
CUBIC_TERM = 0.044715
ROWS = 8
RING_Y, RING_X = 4, 8
PARAMS = pltpu.CompilerParams(vmem_limit_bytes=24 * 1024 * 1024)
VMEM = pl.BlockSpec(memory_space=pltpu.VMEM)
SMEM = pl.BlockSpec(memory_space=pltpu.SMEM)
HBM = pl.BlockSpec(memory_space=pltpu.HBM)


def shape(dims, dtype=jnp.bfloat16):
    return jax.ShapeDtypeStruct(dims, dtype)


def in_hbm(value):
    return pltpu.with_memory_space_constraint(value, pltpu.HBM)


def clip_block(block):
    mean = jnp.sum(jnp.abs(block), axis=1, keepdims=True) * (1.0 / BLOCK)
    scale = (mean + EPSILON).astype(jnp.bfloat16).astype(jnp.float32)
    bound = CLIP_LEVEL * scale
    return jnp.minimum(jnp.maximum(block, -bound), bound).astype(jnp.bfloat16)


def clip_blocks(values):
    return jnp.concatenate(
        [clip_block(values[:, k : k + BLOCK]) for k in range(0, values.shape[1], BLOCK)], axis=1
    )


def weight_kernel(half_ref, quant_hbm, scale_hbm, out_ref, quant_ref, scale_ref, sems):
    fetches = [
        pltpu.make_async_copy(quant_hbm, quant_ref, sems.at[0]),
        pltpu.make_async_copy(scale_hbm, scale_ref, sems.at[1]),
    ]
    for fetch in fetches:
        fetch.start()
    for fetch in fetches:
        fetch.wait()
    own_rows, depth = quant_ref.shape
    width = out_ref.shape[2]
    pieces = depth // 2 // width
    first = half_ref[0] == 0
    scales = scale_ref[...].astype(jnp.float32)
    rows = []
    for r in range(own_rows):
        for c in range(pieces):
            halves = []
            for start in (c * width, depth // 2 + c * width):
                quant = quant_ref[r : r + 1, start : start + width].astype(jnp.float32)
                spread = [
                    jnp.broadcast_to(scales[r : r + 1, k : k + 1], (1, BLOCK))
                    for k in range(start // BLOCK, (start + width) // BLOCK)
                ]
                halves.append(quant * jnp.concatenate(spread, axis=1))
            rows.append(jnp.where(first, halves[0], halves[1]))
    weight = jnp.concatenate(rows, axis=0).astype(jnp.bfloat16)
    for slot in range(out_ref.shape[0]):
        out_ref[slot] = weight


def before_half(half, tokens_ref, rows_ref):
    batch = tokens_ref.shape[0]
    count, width = rows_ref.shape[0] * ROWS, rows_ref.shape[2]
    pieces = ROWS // 2
    weight = rows_ref[...].reshape(count, width)
    which = lax.broadcasted_iota(jnp.int32, (count, 1), 0) % pieces
    total = jnp.zeros((count, batch), jnp.float32)
    for c in range(0, pieces, 2):
        pair = [
            tokens_ref[:, pl.ds(pl.multiple_of((half * pieces + c + k) * width, 128), width)] for k in range(2)
        ]
        product = lax.dot_general(
            weight, jnp.concatenate(pair, axis=0), (((1,), (1,)), ((), ())), preferred_element_type=jnp.float32
        )
        total = total + jnp.where(which == c, product[:, :batch], 0.0)
        total = total + jnp.where(which == c + 1, product[:, batch:], 0.0)
    return jnp.sum(total.reshape(count // pieces, pieces, batch), axis=1)


def own_kernel(half_ref, tokens_ref, rows_ref, out_ref):
    out_ref[...] = before_half(half_ref[0], tokens_ref, rows_ref)


def first_kernel(half_ref, parity_ref, tokens_ref, rows_ref, own_ref, cot_ref, act_ref, slope_ref, sent_ref):
    before = own_ref[...] + before_half(1 - half_ref[0], tokens_ref, rows_ref)
    tanh_inner = jnp.tanh(TANH_SCALE * (before + CUBIC_TERM * before * before * before))
    act_ref[...] = (0.5 * before * (1.0 + tanh_inner)).astype(jnp.bfloat16)
    slope = 0.5 * (1.0 + tanh_inner) + 0.5 * before * (1.0 - tanh_inner * tanh_inner) * TANH_SCALE * (
        1.0 + 3.0 * CUBIC_TERM * before * before
    )
    slope = (cot_ref[...].astype(jnp.float32) * slope).astype(jnp.bfloat16)
    hidden = slope.shape[0]
    to = lax.broadcasted_iota(jnp.int32, (hidden, hidden), 0)
    source = lax.broadcasted_iota(jnp.int32, (hidden, hidden), 1)
    pick = source == to % (hidden // 2) * 2 + to // (hidden // 2)
    slope = jnp.dot(
        jnp.where(pick, 1.0, 0.0).astype(jnp.bfloat16), slope, preferred_element_type=jnp.float32
    ).astype(jnp.bfloat16)
    slope_ref[...] = slope
    partials(slope, tokens_ref, 1 - parity_ref[0], sent_ref)


def second_kernel(parity_ref, tokens_ref, slope_ref, kept_ref):
    partials(slope_ref[...], tokens_ref, parity_ref[0], kept_ref)


def partials(slope, tokens_ref, parity, out_ref):
    slots, nodes, piece = out_ref.shape
    for i in range(slots // 2):
        columns = pl.ds(pl.multiple_of((2 * i + parity) * piece, 128), piece)
        partial = jnp.dot(slope, tokens_ref[:, columns], preferred_element_type=jnp.float32)
        value = clip_blocks(partial)
        out_ref[i] = value[:nodes]
        out_ref[slots // 2 + i] = value[nodes:]


def pair_kernel(kept_ref, got_ref, out_ref):
    for slot in range(out_ref.shape[0]):
        total = kept_ref[slot].astype(jnp.float32) + got_ref[slot].astype(jnp.float32)
        out_ref[slot] = total.astype(jnp.bfloat16)


def group_kernel(got_ref, out_ref):
    total = got_ref[0].astype(jnp.float32)
    for i in range(1, got_ref.shape[0]):
        total = total + got_ref[i].astype(jnp.float32)
    for k in range(out_ref.shape[1]):
        out_ref[:, k, :] = clip_block(total[:, k * BLOCK : (k + 1) * BLOCK])


def per_device(tokens, weight_q, weight_scale, cotangent):
    node_count = lax.axis_size("node")
    local_count = RING_Y * RING_X
    batch, depth = tokens.shape
    own_rows = weight_q.shape[0]
    hidden = cotangent.shape[1]
    piece = hidden * depth // (node_count * local_count)
    half = (lax.axis_index("node") % 2).astype(jnp.int32).reshape(1)
    parity = lax.axis_index("parity").astype(jnp.int32).reshape(1)
    call = functools.partial(pl.pallas_call, compiler_params=PARAMS)

    tokens = pltpu.with_memory_space_constraint(tokens, pltpu.VMEM)
    share = shape((local_count, ROWS, own_rows * depth // 2 // ROWS))
    copies = call(
        weight_kernel,
        out_shape=share,
        in_specs=[SMEM, HBM, HBM],
        out_specs=VMEM,
        scratch_shapes=[
            pltpu.VMEM(weight_q.shape, weight_q.dtype),
            pltpu.VMEM(weight_scale.shape, weight_scale.dtype),
            pltpu.SemaphoreType.DMA((2,)),
        ],
    )(half, in_hbm(weight_q), in_hbm(weight_scale))
    own = lax.all_to_all(copies, ("y", "pair", "parity"), split_axis=0, concat_axis=0, tiled=True)
    other = lax.ppermute(own, "node", [(n, n ^ 1) for n in range(node_count)])
    before = call(
        own_kernel, out_shape=shape((hidden, batch), jnp.float32), in_specs=[SMEM, VMEM, VMEM], out_specs=VMEM
    )(half, tokens, own)
    parts = shape((local_count // 2, node_count, piece))
    activation, slope, sent = call(
        first_kernel,
        out_shape=(shape((hidden, batch)), shape((hidden, batch)), parts),
        in_specs=[SMEM] * 2 + [VMEM] * 4,
        out_specs=(VMEM,) * 3,
    )(half, parity, tokens, other, before, cotangent.T)
    kept = call(second_kernel, out_shape=parts, in_specs=[SMEM, VMEM, VMEM], out_specs=VMEM)(parity, tokens, slope)
    partners = [
        (n * RING_X + x, n * RING_X + (x + (1 if (x + n) % 2 == 0 else -1)) % RING_X)
        for n in range(node_count)
        for x in range(RING_X)
    ]
    paired = lax.ppermute(sent, ("node", "pair", "parity"), partners)
    sent = call(
        pair_kernel, out_shape=parts, in_specs=[VMEM] * 2, out_specs=VMEM
    )(kept, paired)
    got = lax.all_to_all(sent, ("y", "pair"), split_axis=0, concat_axis=0, tiled=True)
    group = call(
        group_kernel, out_shape=shape((node_count, piece // BLOCK, BLOCK)), in_specs=[VMEM], out_specs=VMEM
    )(got)
    got = lax.all_to_all(group, "node", split_axis=0, concat_axis=0, tiled=True)
    gradient = jnp.sum(got.astype(jnp.float32), axis=0)
    return (activation.T, gradient)


def solution(mesh):
    axes = ("node", "y", "pair", "parity")
    fine = Mesh(mesh.devices.reshape(mesh.devices.shape[0], RING_Y, RING_X // 2, 2), axes)
    everywhere, group = P(axes, None), P(axes[1:], None)
    return jax.shard_map(
        per_device,
        mesh=fine,
        in_specs=(everywhere, group, group, everywhere),
        out_specs=(everywhere, everywhere),
        check_vma=False,
    )
```

```python
import functools

import jax
import jax.numpy as jnp
from jax import lax
from jax.experimental import pallas as pl
from jax.experimental.pallas import tpu as pltpu
from jax.sharding import Mesh, PartitionSpec as P

BLOCK = 256
EPSILON = 1e-06
CLIP_LEVEL = 3.0
TANH_SCALE = 0.7978845608028654
CUBIC_TERM = 0.044715
ROWS = 8
RING_Y, RING_X = 4, 8
PARAMS = pltpu.CompilerParams(vmem_limit_bytes=24 * 1024 * 1024)
VMEM = pl.BlockSpec(memory_space=pltpu.VMEM)
SMEM = pl.BlockSpec(memory_space=pltpu.SMEM)
HBM = pl.BlockSpec(memory_space=pltpu.HBM)


def shape(dims, dtype=jnp.bfloat16):
    return jax.ShapeDtypeStruct(dims, dtype)


def in_hbm(value):
    return pltpu.with_memory_space_constraint(value, pltpu.HBM)


def clip_block(block):
    mean = jnp.sum(jnp.abs(block), axis=1, keepdims=True) * (1.0 / BLOCK)
    scale = (mean + EPSILON).astype(jnp.bfloat16).astype(jnp.float32)
    bound = CLIP_LEVEL * scale
    return jnp.minimum(jnp.maximum(block, -bound), bound).astype(jnp.bfloat16)


def clip_blocks(values):
    return jnp.concatenate(
        [clip_block(values[:, k : k + BLOCK]) for k in range(0, values.shape[1], BLOCK)], axis=1
    )


def weight_kernel(half_ref, quant_hbm, scale_hbm, out_ref, quant_ref, scale_ref, sems):
    fetches = [
        pltpu.make_async_copy(quant_hbm, quant_ref, sems.at[0]),
        pltpu.make_async_copy(scale_hbm, scale_ref, sems.at[1]),
    ]
    for fetch in fetches:
        fetch.start()
    for fetch in fetches:
        fetch.wait()
    own_rows, depth = quant_ref.shape
    width = out_ref.shape[2]
    pieces = depth // 2 // width
    first = half_ref[0] == 0
    scales = scale_ref[...].astype(jnp.float32)
    rows = []
    for r in range(own_rows):
        for c in range(pieces):
            halves = []
            for start in (c * width, depth // 2 + c * width):
                quant = quant_ref[r : r + 1, start : start + width].astype(jnp.float32)
                spread = [
                    jnp.broadcast_to(scales[r : r + 1, k : k + 1], (1, BLOCK))
                    for k in range(start // BLOCK, (start + width) // BLOCK)
                ]
                halves.append(quant * jnp.concatenate(spread, axis=1))
            rows.append(jnp.where(first, halves[0], halves[1]))
    weight = jnp.concatenate(rows, axis=0).astype(jnp.bfloat16)
    for slot in range(out_ref.shape[0]):
        out_ref[slot] = weight


def before_half(half, tokens_ref, rows_ref):
    batch = tokens_ref.shape[0]
    count, width = rows_ref.shape[0] * ROWS, rows_ref.shape[2]
    pieces = ROWS // 2
    weight = rows_ref[...].reshape(count, width)
    which = lax.broadcasted_iota(jnp.int32, (count, 1), 0) % pieces
    total = jnp.zeros((count, batch), jnp.float32)
    for c in range(0, pieces, 2):
        pair = [
            tokens_ref[:, pl.ds(pl.multiple_of((half * pieces + c + k) * width, 128), width)] for k in range(2)
        ]
        product = lax.dot_general(
            weight, jnp.concatenate(pair, axis=0), (((1,), (1,)), ((), ())), preferred_element_type=jnp.float32
        )
        total = total + jnp.where(which == c, product[:, :batch], 0.0)
        total = total + jnp.where(which == c + 1, product[:, batch:], 0.0)
    return jnp.sum(total.reshape(count // pieces, pieces, batch), axis=1)


def own_kernel(half_ref, tokens_ref, rows_ref, out_ref):
    out_ref[...] = before_half(half_ref[0], tokens_ref, rows_ref)


def first_kernel(half_ref, parity_ref, tokens_ref, rows_ref, own_ref, cot_ref, before_ref, slope_ref, sent_ref):
    before = own_ref[...] + before_half(1 - half_ref[0], tokens_ref, rows_ref)
    before_ref[...] = before
    tanh_inner = jnp.tanh(TANH_SCALE * (before + CUBIC_TERM * before * before * before))
    slope = 0.5 * (1.0 + tanh_inner) + 0.5 * before * (1.0 - tanh_inner * tanh_inner) * TANH_SCALE * (
        1.0 + 3.0 * CUBIC_TERM * before * before
    )
    slope = (cot_ref[...].astype(jnp.float32) * slope).astype(jnp.bfloat16)
    hidden = slope.shape[0]
    to = lax.broadcasted_iota(jnp.int32, (hidden, hidden), 0)
    source = lax.broadcasted_iota(jnp.int32, (hidden, hidden), 1)
    pick = source == to % (hidden // 2) * 2 + to // (hidden // 2)
    slope = jnp.dot(
        jnp.where(pick, 1.0, 0.0).astype(jnp.bfloat16), slope, preferred_element_type=jnp.float32
    ).astype(jnp.bfloat16)
    slope_ref[...] = slope
    partials(slope, tokens_ref, 1 - parity_ref[0], sent_ref)


def second_kernel(parity_ref, tokens_ref, before_ref, slope_ref, act_ref, kept_ref):
    before = before_ref[...]
    tanh_inner = jnp.tanh(TANH_SCALE * (before + CUBIC_TERM * before * before * before))
    act_ref[...] = (0.5 * before * (1.0 + tanh_inner)).astype(jnp.bfloat16)
    partials(slope_ref[...], tokens_ref, parity_ref[0], kept_ref)


def partials(slope, tokens_ref, parity, out_ref):
    slots, nodes, piece = out_ref.shape
    for i in range(slots // 2):
        columns = pl.ds(pl.multiple_of((2 * i + parity) * piece, 128), piece)
        partial = jnp.dot(slope, tokens_ref[:, columns], preferred_element_type=jnp.float32)
        value = clip_blocks(partial)
        out_ref[i] = value[:nodes]
        out_ref[slots // 2 + i] = value[nodes:]


def pair_kernel(kept_ref, got_ref, out_ref):
    for slot in range(out_ref.shape[0]):
        total = kept_ref[slot].astype(jnp.float32) + got_ref[slot].astype(jnp.float32)
        out_ref[slot] = total.astype(jnp.bfloat16)


def group_kernel(got_ref, out_ref):
    total = got_ref[0].astype(jnp.float32)
    for i in range(1, got_ref.shape[0]):
        total = total + got_ref[i].astype(jnp.float32)
    for k in range(out_ref.shape[1]):
        out_ref[:, k, :] = clip_block(total[:, k * BLOCK : (k + 1) * BLOCK])


def per_device(tokens, weight_q, weight_scale, cotangent):
    node_count = lax.axis_size("node")
    local_count = RING_Y * RING_X
    batch, depth = tokens.shape
    own_rows = weight_q.shape[0]
    hidden = cotangent.shape[1]
    piece = hidden * depth // (node_count * local_count)
    half = (lax.axis_index("node") % 2).astype(jnp.int32).reshape(1)
    parity = lax.axis_index("parity").astype(jnp.int32).reshape(1)
    call = functools.partial(pl.pallas_call, compiler_params=PARAMS)

    tokens = pltpu.with_memory_space_constraint(tokens, pltpu.VMEM)
    share = shape((local_count, ROWS, own_rows * depth // 2 // ROWS))
    copies = call(
        weight_kernel,
        out_shape=share,
        in_specs=[SMEM, HBM, HBM],
        out_specs=VMEM,
        scratch_shapes=[
            pltpu.VMEM(weight_q.shape, weight_q.dtype),
            pltpu.VMEM(weight_scale.shape, weight_scale.dtype),
            pltpu.SemaphoreType.DMA((2,)),
        ],
    )(half, in_hbm(weight_q), in_hbm(weight_scale))
    own = lax.all_to_all(copies, ("y", "pair", "parity"), split_axis=0, concat_axis=0, tiled=True)
    other = lax.ppermute(own, "node", [(n, n ^ 1) for n in range(node_count)])
    before = call(
        own_kernel, out_shape=shape((hidden, batch), jnp.float32), in_specs=[SMEM, VMEM, VMEM], out_specs=VMEM
    )(half, tokens, own)
    parts = shape((local_count // 2, node_count, piece))
    before, slope, sent = call(
        first_kernel,
        out_shape=(shape((hidden, batch), jnp.float32), shape((hidden, batch)), parts),
        in_specs=[SMEM] * 2 + [VMEM] * 4,
        out_specs=(VMEM,) * 3,
    )(half, parity, tokens, other, before, cotangent.T)
    activation, kept = call(
        second_kernel,
        out_shape=(shape((hidden, batch)), parts),
        in_specs=[SMEM] + [VMEM] * 3,
        out_specs=(VMEM,) * 2,
    )(parity, tokens, before, slope)
    partners = [
        (n * RING_X + x, n * RING_X + (x + (1 if (x + n) % 2 == 0 else -1)) % RING_X)
        for n in range(node_count)
        for x in range(RING_X)
    ]
    paired = lax.ppermute(sent, ("node", "pair", "parity"), partners)
    sent = call(
        pair_kernel, out_shape=parts, in_specs=[VMEM] * 2, out_specs=VMEM
    )(kept, paired)
    got = lax.all_to_all(sent, ("y", "pair"), split_axis=0, concat_axis=0, tiled=True)
    group = call(
        group_kernel, out_shape=shape((node_count, piece // BLOCK, BLOCK)), in_specs=[VMEM], out_specs=VMEM
    )(got)
    got = lax.all_to_all(group, "node", split_axis=0, concat_axis=0, tiled=True)
    gradient = jnp.sum(got.astype(jnp.float32), axis=0)
    return (activation.T, gradient)


def solution(mesh):
    axes = ("node", "y", "pair", "parity")
    fine = Mesh(mesh.devices.reshape(mesh.devices.shape[0], RING_Y, RING_X // 2, 2), axes)
    everywhere, group = P(axes, None), P(axes[1:], None)
    return jax.shard_map(
        per_device,
        mesh=fine,
        in_specs=(everywhere, group, group, everywhere),
        out_specs=(everywhere, everywhere),
        check_vma=False,
    )
```

```python
import functools

import jax
import jax.numpy as jnp
from jax import lax
from jax.experimental import pallas as pl
from jax.experimental.pallas import tpu as pltpu
from jax.sharding import Mesh, PartitionSpec as P

BLOCK = 256
EPSILON = 1e-06
CLIP_LEVEL = 3.0
TANH_SCALE = 0.7978845608028654
CUBIC_TERM = 0.044715
ROWS = 8
RING_Y, RING_X = 4, 8
PARAMS = pltpu.CompilerParams(vmem_limit_bytes=24 * 1024 * 1024)
VMEM = pl.BlockSpec(memory_space=pltpu.VMEM)
SMEM = pl.BlockSpec(memory_space=pltpu.SMEM)
HBM = pl.BlockSpec(memory_space=pltpu.HBM)


def shape(dims, dtype=jnp.bfloat16):
    return jax.ShapeDtypeStruct(dims, dtype)


def in_hbm(value):
    return pltpu.with_memory_space_constraint(value, pltpu.HBM)


def clip_block(block):
    mean = jnp.sum(jnp.abs(block), axis=1, keepdims=True) * (1.0 / BLOCK)
    scale = (mean + EPSILON).astype(jnp.bfloat16).astype(jnp.float32)
    bound = CLIP_LEVEL * scale
    return jnp.minimum(jnp.maximum(block, -bound), bound).astype(jnp.bfloat16)


def clip_blocks(values):
    return jnp.concatenate(
        [clip_block(values[:, k : k + BLOCK]) for k in range(0, values.shape[1], BLOCK)], axis=1
    )


def weight_kernel(half_ref, quant_hbm, scale_hbm, out_ref, quant_ref, scale_ref, sems):
    fetches = [
        pltpu.make_async_copy(quant_hbm, quant_ref, sems.at[0]),
        pltpu.make_async_copy(scale_hbm, scale_ref, sems.at[1]),
    ]
    for fetch in fetches:
        fetch.start()
    for fetch in fetches:
        fetch.wait()
    own_rows, depth = quant_ref.shape
    width = out_ref.shape[2]
    pieces = depth // 2 // width
    first = half_ref[0] == 0
    scales = scale_ref[...].astype(jnp.float32)
    rows = []
    for r in range(own_rows):
        for c in range(pieces):
            halves = []
            for start in (c * width, depth // 2 + c * width):
                quant = quant_ref[r : r + 1, start : start + width].astype(jnp.float32)
                spread = [
                    jnp.broadcast_to(scales[r : r + 1, k : k + 1], (1, BLOCK))
                    for k in range(start // BLOCK, (start + width) // BLOCK)
                ]
                halves.append(quant * jnp.concatenate(spread, axis=1))
            rows.append(jnp.where(first, halves[0], halves[1]))
    weight = jnp.concatenate(rows, axis=0).astype(jnp.bfloat16)
    for slot in range(out_ref.shape[0]):
        out_ref[slot] = weight


def before_half(half, tokens_ref, rows_ref):
    batch = tokens_ref.shape[0]
    count, width = rows_ref.shape[0] * ROWS, rows_ref.shape[2]
    pieces = ROWS // 2
    weight = rows_ref[...].reshape(count, width)
    which = lax.broadcasted_iota(jnp.int32, (count, 1), 0) % pieces
    total = jnp.zeros((count, batch), jnp.float32)
    for c in range(0, pieces, 2):
        pair = [
            tokens_ref[:, pl.ds(pl.multiple_of((half * pieces + c + k) * width, 128), width)] for k in range(2)
        ]
        product = lax.dot_general(
            weight, jnp.concatenate(pair, axis=0), (((1,), (1,)), ((), ())), preferred_element_type=jnp.float32
        )
        total = total + jnp.where(which == c, product[:, :batch], 0.0)
        total = total + jnp.where(which == c + 1, product[:, batch:], 0.0)
    total = total.reshape(count // ROWS, ROWS, batch)
    return jnp.concatenate([jnp.sum(total[:, :pieces], axis=1), jnp.sum(total[:, pieces:], axis=1)], axis=0)


def reorder(rows, back):
    count = rows.shape[0]
    number = lax.broadcasted_iota(jnp.int32, (count, count), 0 if back else 1)
    place = lax.broadcasted_iota(jnp.int32, (count, count), 1 if back else 0)
    pick = jnp.where(number == place % (count // 2) * 2 + place // (count // 2), 1.0, 0.0).astype(jnp.bfloat16)
    return jnp.dot(pick, rows, preferred_element_type=jnp.float32).astype(jnp.bfloat16)


def own_kernel(half_ref, tokens_ref, rows_ref, cot_ref, out_ref, sorted_ref):
    sorted_ref[...] = reorder(cot_ref[...], False)
    out_ref[...] = before_half(half_ref[0], tokens_ref, rows_ref)


def first_kernel(half_ref, parity_ref, tokens_ref, rows_ref, own_ref, cot_ref, before_ref, slope_ref, sent_ref):
    before = own_ref[...] + before_half(1 - half_ref[0], tokens_ref, rows_ref)
    before_ref[...] = before
    tanh_inner = jnp.tanh(TANH_SCALE * (before + CUBIC_TERM * before * before * before))
    slope = 0.5 * (1.0 + tanh_inner) + 0.5 * before * (1.0 - tanh_inner * tanh_inner) * TANH_SCALE * (
        1.0 + 3.0 * CUBIC_TERM * before * before
    )
    slope = (cot_ref[...].astype(jnp.float32) * slope).astype(jnp.bfloat16)
    slope_ref[...] = slope
    partials(slope, tokens_ref, 1 - parity_ref[0], sent_ref)


def second_kernel(parity_ref, tokens_ref, before_ref, slope_ref, act_ref, kept_ref):
    before = before_ref[...]
    tanh_inner = jnp.tanh(TANH_SCALE * (before + CUBIC_TERM * before * before * before))
    act_ref[...] = reorder((0.5 * before * (1.0 + tanh_inner)).astype(jnp.bfloat16), True)
    partials(slope_ref[...], tokens_ref, parity_ref[0], kept_ref)


def partials(slope, tokens_ref, parity, out_ref):
    slots, nodes, piece = out_ref.shape
    for i in range(slots // 2):
        columns = pl.ds(pl.multiple_of((2 * i + parity) * piece, 128), piece)
        partial = jnp.dot(slope, tokens_ref[:, columns], preferred_element_type=jnp.float32)
        value = clip_blocks(partial)
        out_ref[i] = value[:nodes]
        out_ref[slots // 2 + i] = value[nodes:]


def pair_kernel(kept_ref, got_ref, out_ref):
    for slot in range(out_ref.shape[0]):
        total = kept_ref[slot].astype(jnp.float32) + got_ref[slot].astype(jnp.float32)
        out_ref[slot] = total.astype(jnp.bfloat16)


def group_kernel(got_ref, out_ref):
    total = got_ref[0].astype(jnp.float32)
    for i in range(1, got_ref.shape[0]):
        total = total + got_ref[i].astype(jnp.float32)
    for k in range(out_ref.shape[1]):
        out_ref[:, k, :] = clip_block(total[:, k * BLOCK : (k + 1) * BLOCK])


def per_device(tokens, weight_q, weight_scale, cotangent):
    node_count = lax.axis_size("node")
    local_count = RING_Y * RING_X
    batch, depth = tokens.shape
    own_rows = weight_q.shape[0]
    hidden = cotangent.shape[1]
    piece = hidden * depth // (node_count * local_count)
    half = (lax.axis_index("node") % 2).astype(jnp.int32).reshape(1)
    parity = lax.axis_index("parity").astype(jnp.int32).reshape(1)
    call = functools.partial(pl.pallas_call, compiler_params=PARAMS)

    tokens = pltpu.with_memory_space_constraint(tokens, pltpu.VMEM)
    share = shape((local_count, ROWS, own_rows * depth // 2 // ROWS))
    copies = call(
        weight_kernel,
        out_shape=share,
        in_specs=[SMEM, HBM, HBM],
        out_specs=VMEM,
        scratch_shapes=[
            pltpu.VMEM(weight_q.shape, weight_q.dtype),
            pltpu.VMEM(weight_scale.shape, weight_scale.dtype),
            pltpu.SemaphoreType.DMA((2,)),
        ],
    )(half, in_hbm(weight_q), in_hbm(weight_scale))
    own = lax.all_to_all(copies, ("y", "pair", "parity"), split_axis=0, concat_axis=0, tiled=True)
    other = lax.ppermute(own, "node", [(n, n ^ 1) for n in range(node_count)])
    before, sorted_cot = call(
        own_kernel,
        out_shape=(shape((hidden, batch), jnp.float32), shape((hidden, batch))),
        in_specs=[SMEM] + [VMEM] * 3,
        out_specs=(VMEM, VMEM),
    )(half, tokens, own, cotangent.T)
    parts = shape((local_count // 2, node_count, piece))
    before, slope, sent = call(
        first_kernel,
        out_shape=(shape((hidden, batch), jnp.float32), shape((hidden, batch)), parts),
        in_specs=[SMEM] * 2 + [VMEM] * 4,
        out_specs=(VMEM,) * 3,
    )(half, parity, tokens, other, before, sorted_cot)
    activation, kept = call(
        second_kernel,
        out_shape=(shape((hidden, batch)), parts),
        in_specs=[SMEM] + [VMEM] * 3,
        out_specs=(VMEM,) * 2,
    )(parity, tokens, before, slope)
    partners = [
        (n * RING_X + x, n * RING_X + (x + (1 if (x + n) % 2 == 0 else -1)) % RING_X)
        for n in range(node_count)
        for x in range(RING_X)
    ]
    paired = lax.ppermute(sent, ("node", "pair", "parity"), partners)
    sent = call(
        pair_kernel, out_shape=parts, in_specs=[VMEM] * 2, out_specs=VMEM
    )(kept, paired)
    got = lax.all_to_all(sent, ("y", "pair"), split_axis=0, concat_axis=0, tiled=True)
    group = call(
        group_kernel, out_shape=shape((node_count, piece // BLOCK, BLOCK)), in_specs=[VMEM], out_specs=VMEM
    )(got)
    got = lax.all_to_all(group, "node", split_axis=0, concat_axis=0, tiled=True)
    gradient = jnp.sum(got.astype(jnp.float32), axis=0)
    return (activation.T, gradient)


def solution(mesh):
    axes = ("node", "y", "pair", "parity")
    fine = Mesh(mesh.devices.reshape(mesh.devices.shape[0], RING_Y, RING_X // 2, 2), axes)
    everywhere, group = P(axes, None), P(axes[1:], None)
    return jax.shard_map(
        per_device,
        mesh=fine,
        in_specs=(everywhere, group, group, everywhere),
        out_specs=(everywhere, everywhere),
        check_vma=False,
    )
```
